32 devices in a mesh: section: 8 (over y, x, core), dp: 4 (over z).
Axes of the slice: x: 2, y: 2, z: 4, core: 2. Of those that a mesh axis runs over, the one named last changes fastest.
Arguments:
- tokens: bfloat16 [6144, 4096], P(('section', 'dp')), may hold values from -6 to 6
- cotangent: bfloat16 [6144, 4096], P(('section', 'dp')), may hold values from -0.09375 to 0.09375
- gate_weight: bfloat16 [256, 4096], P('section'), may hold values from -0.09375 to 0.09375
- up_weight: bfloat16 [256, 4096], P('section'), may hold values from -0.09375 to 0.09375
- down_weight: bfloat16 [256, 4096], P('section'), may hold values from -0.375 to 0.375
Outputs:
- grad_gate: bfloat16 [256, 4096], P('section')
- grad_up: bfloat16 [256, 4096], P('section')
- grad_down: bfloat16 [256, 4096], P('section')
The draws below stay inside these ranges and needn't reach their ends.
All inputs are finite; a program needn't handle non-finite values.
Results may differ from the reference program's by a relative error of at most 0.0051.
Values may be sent and summed in bfloat16 or wider, within the bound.
No kernel may reach another device: no remote copies, remote signals or barrier semaphores. Data moves between devices by JAX's collectives and lax.ppermute only.
A program may use at most 64 MiB of HBM per device.

```python
import jax
import jax.numpy as jnp
from jax import lax

D = 4096
BLOCK = 32
STEPS = 6
TOK = 192
FFW = 256
TOKENS = 6144
N_SECTION = 8
N_DP = 4


def level_of(stream_key, shape, cuts, low, largest):
    factor_of, own = 1.0, jax.random.fold_in(stream_key, 6)
    for axis_at, parts in cuts:
        draws = jnp.exp(jax.random.uniform(jax.random.fold_in(own, axis_at), (parts,), jnp.float32, low / len(cuts), largest / len(cuts)))
        factor_of = factor_of * jnp.repeat(draws, shape[axis_at] // parts).reshape([-1 if axis == axis_at else 1 for axis in range(len(shape))])
    return factor_of


def scatter_about(rng, shape, width, most, cuts=(), kind=jnp.bfloat16):
    array = jax.random.normal(rng, shape, jnp.float32) * width
    if len(cuts) > 0:
        array = level_of(rng, shape, cuts, -0.22, 0.18) * array
    return jnp.clip(array, min=-most, max=most).astype(kind)


def setup_inputs(seed: int = 0) -> dict:
    streams_of = jax.random.split(jax.random.key(seed), 6)
    return {
        "tokens": scatter_about(streams_of[0], (TOKENS, D), 1.0, 6.0, ((0, 32),)),
        "cotangent": scatter_about(streams_of[1], (TOKENS, D), (TOK * STEPS * N_DP) ** -0.5, 0.09375, ((0, 32),)),
        "gate_weight": scatter_about(streams_of[2], (FFW, D), D ** -0.5, 0.09375, ((0, 8),)),
        "up_weight": scatter_about(streams_of[3], (FFW, D), D ** -0.5, 0.09375, ((0, 8),)),
        "down_weight": scatter_about(streams_of[4], (FFW, D), FFW ** -0.5, 0.375, ((0, 8),)),
    }


def contract(left, right):
    return lax.dot_general(left, right, (((1,), (1,)), ((), ())), preferred_element_type=jnp.float32)


def block_grads(rows, cotangent_rows, gate, upper, down):
    gate_sum = contract(gate, rows)
    up_sum = contract(upper, rows)
    squash = jax.nn.sigmoid(gate_sum)
    activated = gate_sum * squash
    hidden = (activated * up_sum).astype(jnp.bfloat16)
    backward = contract(down, cotangent_rows)
    gate_back = (backward * up_sum * squash * (1.0 + gate_sum * (1.0 - squash))).astype(jnp.bfloat16)
    up_back = (backward * activated).astype(jnp.bfloat16)
    return (jnp.dot(gate_back, rows, preferred_element_type=jnp.float32),
            jnp.dot(up_back, rows, preferred_element_type=jnp.float32),
            jnp.dot(hidden, cotangent_rows, preferred_element_type=jnp.float32))


def reference(tokens, cotangent, gate_weight, up_weight, down_weight):
    stacked_rows = tokens.reshape(N_SECTION, N_DP * TOK, D)
    stacked_back = cotangent.reshape(N_SECTION, N_DP * TOK, D)
    gates = gate_weight.reshape(N_SECTION, BLOCK, D)
    uppers = up_weight.reshape(N_SECTION, BLOCK, D)
    downs = down_weight.reshape(N_SECTION, BLOCK, D)

    def one_block(block_id):
        picks = (block_id + jnp.arange(STEPS, dtype=jnp.int32)) % N_SECTION
        rows = jnp.take(stacked_rows, picks, axis=0).reshape(STEPS * N_DP * TOK, D)
        cotangent_rows = jnp.take(stacked_back, picks, axis=0).reshape(STEPS * N_DP * TOK, D)
        gate = lax.dynamic_index_in_dim(gates, block_id, 0, keepdims=False)
        upper = lax.dynamic_index_in_dim(uppers, block_id, 0, keepdims=False)
        down = lax.dynamic_index_in_dim(downs, block_id, 0, keepdims=False)
        return block_grads(rows, cotangent_rows, gate, upper, down)

    sums = lax.map(one_block, jnp.arange(N_SECTION, dtype=jnp.int32))
    placed = [jnp.roll(summed, STEPS - 1, axis=0).reshape(FFW, D).astype(jnp.bfloat16) for summed in sums]
    return (placed[0], placed[1], placed[2])
```

```python
import jax
import jax.numpy as jnp
from jax import lax
from jax.sharding import PartitionSpec as P

STEPS = 6
F32 = jnp.float32
BF16 = jnp.bfloat16


def from_behind(block, axis, distance):
    devices = range(lax.axis_size(axis))
    route = [((i - distance) % len(devices), i) for i in devices]
    return lax.ppermute(block, axis, route)


def contract(left, right):
    return lax.dot_general(
        left, right, (((1,), (1,)), ((), ())), preferred_element_type=F32
    )


def rows_dot(left, right):
    return jnp.dot(left, right, preferred_element_type=F32)


def activations(tokens, cotangent, gate, upper, down):
    gate_sum = contract(gate, tokens)
    up_sum = contract(upper, tokens)
    squash = jax.nn.sigmoid(gate_sum)
    activated = gate_sum * squash
    hidden = (activated * up_sum).astype(BF16)
    backward = contract(down, cotangent)
    gate_back = (backward * up_sum * squash * (1.0 + gate_sum * (1.0 - squash))).astype(
        BF16
    )
    up_back = (backward * activated).astype(BF16)
    return gate_back, up_back, hidden


def ring(tokens, cotangent, gate_weight, up_weight, down_weight):
    held = jnp.stack([gate_weight, up_weight, down_weight])
    summed = None
    for position in range(STEPS):
        if position > 0:
            held = from_behind(held, "section", 1)
        parts = activations(tokens, cotangent, held[0], held[1], held[2])
        piece = jnp.stack(
            [
                rows_dot(parts[0], tokens),
                rows_dot(parts[1], tokens),
                rows_dot(parts[2], cotangent),
            ]
        )
        if position > 0:
            summed = from_behind(summed, "section", 1) + piece
        else:
            summed = piece
    finished = lax.psum(summed, "dp").astype(BF16)
    return (finished[0], finished[1], finished[2])


def flip(block, mask):
    return lax.ppermute(block, "section", [(i, i ^ mask) for i in range(8)])


def along(block, route):
    return lax.ppermute(block, "dp", route)


CORE, X, Y = 1, 2, 4
COLUMN_PARTS = 2


def square(tokens, cotangent, gate_weight, up_weight, down_weight):
    section = lax.axis_index("section")
    core = section % 2
    chip = section // 2
    line = lax.axis_index("dp")
    block = gate_weight.shape[0]
    half = block // 2
    tok = tokens.shape[0]
    width = tokens.shape[1]

    tokens2 = jnp.concatenate([tokens, flip(tokens, CORE)])
    cotangent2 = jnp.concatenate([cotangent, flip(cotangent, CORE)])

    own = [gate_weight, up_weight, down_weight]
    from_x = [flip(w, X) for w in own]
    from_y = [flip(w, Y) for w in own]
    diagonal = [
        jnp.concatenate([flip(fy[:half], X), flip(fx[half:], Y)])
        for fx, fy in zip(from_x, from_y)
    ]

    sections2 = jnp.repeat(jnp.stack([section, section ^ 1]), tok)

    def masked(parts, chips):
        blocks = jnp.repeat(jnp.stack([2 * c + core for c in chips]), block)
        meets = (sections2[None, :] - blocks[:, None]) % 8 < STEPS
        return [jnp.where(meets, part, 0).astype(BF16) for part in parts]

    near = [jnp.concatenate([o, x, y]) for o, x, y in zip(own, from_x, from_y)]
    near = masked(
        activations(tokens2, cotangent2, *near), [chip, chip ^ 1, chip ^ 2]
    )
    far = masked(activations(tokens2, cotangent2, *diagonal), [chip ^ 3])
    even_core = core == 0
    even_chip = chip % 2 == 0

    def pick(a, b, c):
        return jnp.where(even_core, a, jnp.where(even_chip, b, c))

    sources = [tokens2, tokens2, cotangent2]
    to_diagonal = []
    rest = []
    for part, last in zip(near, far):
        o, x, y = part[:block], part[block : 2 * block], part[2 * block :]
        to_diagonal.append(pick(x, o, y))
        rest.append(
            jnp.concatenate([pick(last, y, o), pick(o, last, x), pick(y, x, last)])
        )

    relayed = []
    for left, right in zip(to_diagonal, sources):
        sums = rows_dot(left, right).astype(BF16)
        relayed.append((flip(sums[:half], X), flip(sums[half:], Y)))

    step = width // COLUMN_PARTS
    results = []
    for at in range(3):
        row = []
        for part in range(COLUMN_PARTS):
            columns = slice(part * step, (part + 1) * step)
            sums = rows_dot(rest[at], sources[at][:, columns])
            via_x, via_y = relayed[at]
            to_x = jnp.concatenate(
                [sums[:half], sums[half:block] + via_y[:, columns].astype(F32)]
            ).astype(BF16)
            to_y = jnp.concatenate(
                [
                    sums[block : block + half] + via_x[:, columns].astype(F32),
                    sums[block + half : 2 * block],
                ]
            ).astype(BF16)
            stay = flip(sums[2 * block :].astype(BF16), CORE)
            total = (
                flip(to_x, X | CORE).astype(F32)
                + flip(to_y, Y | CORE).astype(F32)
                + stay.astype(F32)
            )
            inward = along(total.astype(BF16), [(0, 1), (3, 2)])
            pair = lax.reduce_precision(total + inward.astype(F32), 8, 7)
            across = along(pair.astype(BF16), [(1, 2), (2, 1)])
            done = (pair + across.astype(F32)).astype(BF16)
            outward = along(done, [(1, 0), (2, 3)])
            row.append(jnp.where((line == 1) | (line == 2), done, outward))
        results.append(jnp.concatenate(row, axis=1))
    return tuple(results)


def solution(mesh):
    fits = mesh.shape["section"] == 8 and mesh.shape["dp"] == 4
    return jax.shard_map(
        square if fits else ring,
        mesh=mesh,
        in_specs=(
            P(("section", "dp"), None),
            P(("section", "dp"), None),
            P("section", None),
            P("section", None),
            P("section", None),
        ),
        out_specs=(P("section", None), P("section", None), P("section", None)),
        check_vma=False,
    )
```

```python
import jax
import jax.numpy as jnp
from jax import lax
from jax.sharding import PartitionSpec as P

STEPS = 6
F32 = jnp.float32
BF16 = jnp.bfloat16


def from_behind(block, axis, distance):
    devices = range(lax.axis_size(axis))
    route = [((i - distance) % len(devices), i) for i in devices]
    return lax.ppermute(block, axis, route)


def contract(left, right):
    return lax.dot_general(
        left, right, (((1,), (1,)), ((), ())), preferred_element_type=F32
    )


def rows_dot(left, right):
    return jnp.dot(left, right, preferred_element_type=F32)


def activations(tokens, cotangent, gate, upper, down):
    gate_sum = contract(gate, tokens)
    up_sum = contract(upper, tokens)
    squash = jax.nn.sigmoid(gate_sum)
    activated = gate_sum * squash
    hidden = (activated * up_sum).astype(BF16)
    backward = contract(down, cotangent)
    gate_back = (backward * up_sum * squash * (1.0 + gate_sum * (1.0 - squash))).astype(
        BF16
    )
    up_back = (backward * activated).astype(BF16)
    return gate_back, up_back, hidden


def ring(tokens, cotangent, gate_weight, up_weight, down_weight):
    held = jnp.stack([gate_weight, up_weight, down_weight])
    summed = None
    for position in range(STEPS):
        if position > 0:
            held = from_behind(held, "section", 1)
        parts = activations(tokens, cotangent, held[0], held[1], held[2])
        piece = jnp.stack(
            [
                rows_dot(parts[0], tokens),
                rows_dot(parts[1], tokens),
                rows_dot(parts[2], cotangent),
            ]
        )
        if position > 0:
            summed = from_behind(summed, "section", 1) + piece
        else:
            summed = piece
    finished = lax.psum(summed, "dp").astype(BF16)
    return (finished[0], finished[1], finished[2])


def hop(block, step, only=None):
    route = [(i, i ^ step(i)) for i in range(8) if only is None or i % 2 == only]
    return lax.ppermute(block, "section", route)


def along(block, route):
    return lax.ppermute(block, "dp", route)


CORE, X, Y = 1, 2, 4
PAIRS = [(0, 1), (1, 0), (2, 3), (3, 2)]
ACROSS = [(0, 3), (3, 0), (1, 2), (2, 1)]


def after(value, *others):
    return lax.optimization_barrier((value, others))[0]


def square(tokens, cotangent, gate_weight, up_weight, down_weight):
    section = lax.axis_index("section")
    core = section % 2
    chip = section // 2
    line = lax.axis_index("dp")
    block = gate_weight.shape[0]
    half = block // 2
    tok = tokens.shape[0]
    first = core == 0
    even = chip % 2 == 0
    keep_low = jnp.logical_or(line == 0, line == 3)

    def spread(own):
        v = [(i, i ^ (Y | CORE if i % 4 == 2 else CORE)) for i in range(8)]
        u = [
            (i, i ^ (X | CORE if i % 2 else (Y | CORE if i % 4 == 0 else CORE)))
            for i in range(8)
        ]
        return lax.ppermute(own, "section", v), lax.ppermute(own, "section", u)

    def other(i):
        return Y if i % 2 == 0 else X

    gu = jnp.stack([gate_weight, up_weight]).reshape(2 * block, -1)
    gu_v, gu_u = spread(gu)
    tokens_in = hop(after(tokens, gu), lambda i: CORE)
    dn_v, dn_u = spread(after(down_weight, gu))
    cotangent_in = hop(after(cotangent, gu), lambda i: CORE)
    gu_s = hop(gu_v, other)
    dn_s = hop(dn_v, other)

    tokens2 = jnp.concatenate([tokens, tokens_in])
    cotangent2 = jnp.concatenate([cotangent, cotangent_in])

    swapped = jnp.logical_and(core == 1, chip % 2 == 1)
    next_chip = jnp.where(first, chip ^ 1, chip ^ 2)
    sections = jnp.concatenate(
        [jnp.full((1, tok), section), jnp.full((1, tok), section ^ 1)], axis=1
    )

    def forward_half(weights, holder):
        sums = contract(weights, tokens2)
        gate_sum, up_sum = sums[:block], sums[block:]
        squash = jax.nn.sigmoid(gate_sum)
        activated = gate_sum * squash
        meets = (sections - (2 * holder + 1 - core)) % 8 < STEPS
        hidden = jnp.where(meets, activated * up_sum, 0).astype(BF16)
        slope = up_sum * squash * (1.0 + gate_sum * (1.0 - squash))
        return hidden, jnp.where(meets, slope, 0), jnp.where(meets, activated, 0)

    def backward_half(weights, found):
        backward = contract(weights, cotangent2)
        return jnp.concatenate(
            [(backward * found[1]).astype(BF16), (backward * found[2]).astype(BF16)]
        )

    def spots(v, u, e):
        z = jnp.where(first, e, v)
        return jnp.concatenate([jnp.where(even, z, u), jnp.where(even, u, z)])

    fv = forward_half(gu_v, jnp.where(swapped, next_chip, chip))
    fu = forward_half(gu_u, jnp.where(swapped, chip, next_chip))
    gu_e = hop(after(gu_u, fv), lambda i: Y, 0)
    down_p = hop(rows_dot(fv[0], cotangent2).astype(BF16), lambda i: X, 0)
    bv = backward_half(dn_v, fv)
    bu = backward_half(dn_u, fu)
    dn_e = hop(after(dn_u, bv), lambda i: Y, 0)
    both_p = hop(rows_dot(bv, tokens2).astype(BF16), lambda i: X, 0)

    fs = forward_half(gu_s, jnp.where(first, chip ^ 2, (chip + 3) % 4))
    down_q = hop(rows_dot(fs[0], cotangent2).astype(BF16), lambda i: X)
    bs = backward_half(dn_s, fs)
    sums_q = rows_dot(bs, tokens2).astype(BF16)
    gate_q = hop(sums_q[:block], lambda i: X)
    up_q = hop(sums_q[block:], lambda i: X)

    fe = forward_half(gu_e, chip ^ 3)
    down_r = rows_dot(spots(fv[0], fu[0], fe[0]), cotangent2)
    be = backward_half(dn_e, fe)
    both_r = rows_dot(spots(bv, bu, be), tokens2)

    def reduced(p, q, leaving, staying):
        p, q = p.astype(F32), q.astype(F32)
        leaving = leaving + jnp.where(even, q, p)
        r = hop(leaving.astype(BF16), lambda i: Y)
        total = staying + jnp.where(even, p, q) + r.astype(F32)
        low, high = total[:half], total[half:]
        other = along(jnp.where(keep_low, high, low).astype(BF16), PAIRS)
        kept = jnp.where(keep_low, low, high) + other.astype(F32)
        kept = lax.reduce_precision(kept, 8, 7)
        done = (kept + along(kept.astype(BF16), ACROSS).astype(F32)).astype(BF16)
        back = along(done, PAIRS)
        return jnp.concatenate(
            [jnp.where(keep_low, done, back), jnp.where(keep_low, back, done)]
        )

    grad_down = reduced(down_p, down_q, down_r[:block], down_r[block:])
    part = [both_r[at * block : (at + 1) * block] for at in range(4)]
    grad_gate = reduced(both_p[:block], gate_q, part[0], part[2])
    grad_up = reduced(both_p[block:], up_q, part[1], part[3])
    return grad_gate, grad_up, grad_down


def solution(mesh):
    fits = mesh.shape["section"] == 8 and mesh.shape["dp"] == 4
    return jax.shard_map(
        square if fits else ring,
        mesh=mesh,
        in_specs=(
            P(("section", "dp"), None),
            P(("section", "dp"), None),
            P("section", None),
            P("section", None),
            P("section", None),
        ),
        out_specs=(P("section", None), P("section", None), P("section", None)),
        check_vma=False,
    )
```

```python
import jax
import jax.numpy as jnp
from jax import lax
from jax.experimental import pallas as pl
from jax.experimental.pallas import tpu as pltpu
from jax.sharding import PartitionSpec as P

STEPS = 6
F32 = jnp.float32
BF16 = jnp.bfloat16


def from_behind(block, axis, distance):
    devices = range(lax.axis_size(axis))
    route = [((i - distance) % len(devices), i) for i in devices]
    return lax.ppermute(block, axis, route)


def contract(left, right):
    return lax.dot_general(
        left, right, (((1,), (1,)), ((), ())), preferred_element_type=F32
    )


def rows_dot(left, right):
    return jnp.dot(left, right, preferred_element_type=F32)


def activations(tokens, cotangent, gate, upper, down):
    gate_sum = contract(gate, tokens)
    up_sum = contract(upper, tokens)
    squash = jax.nn.sigmoid(gate_sum)
    activated = gate_sum * squash
    hidden = (activated * up_sum).astype(BF16)
    backward = contract(down, cotangent)
    gate_back = (backward * up_sum * squash * (1.0 + gate_sum * (1.0 - squash))).astype(
        BF16
    )
    up_back = (backward * activated).astype(BF16)
    return gate_back, up_back, hidden


def ring(tokens, cotangent, gate_weight, up_weight, down_weight):
    held = jnp.stack([gate_weight, up_weight, down_weight])
    summed = None
    for position in range(STEPS):
        if position > 0:
            held = from_behind(held, "section", 1)
        parts = activations(tokens, cotangent, held[0], held[1], held[2])
        piece = jnp.stack(
            [
                rows_dot(parts[0], tokens),
                rows_dot(parts[1], tokens),
                rows_dot(parts[2], cotangent),
            ]
        )
        if position > 0:
            summed = from_behind(summed, "section", 1) + piece
        else:
            summed = piece
    finished = lax.psum(summed, "dp").astype(BF16)
    return (finished[0], finished[1], finished[2])


def hop(block, step, only=None):
    route = [(i, i ^ step(i)) for i in range(8) if only is None or i % 2 == only]
    return lax.ppermute(block, "section", route)


def along(block, route):
    return lax.ppermute(block, "dp", route)


CORE, X, Y = 1, 2, 4
PAIRS = [(0, 1), (1, 0), (2, 3), (3, 2)]
ACROSS = [(0, 3), (3, 0), (1, 2), (2, 1)]
SPAN = 512
VMEM_LIMIT = 8 * 2**20


def after(value, *others):
    return lax.optimization_barrier((value, others))[0]


def on_chip(*parts):
    def kernel(*refs):
        sources, out, sems = refs[: len(parts)], refs[-2], refs[-1]
        copies, row = [], 0
        for at, source in enumerate(sources):
            rows = source.shape[0]
            spot = out.at[pl.ds(row, rows)]
            copies.append(pltpu.make_async_copy(source, spot, sems.at[at]))
            row += rows
        for copy in copies:
            copy.start()
        for copy in copies:
            copy.wait()

    rows = sum(part.shape[0] for part in parts)
    return pl.pallas_call(
        kernel,
        out_shape=pltpu.VMEM((rows, parts[0].shape[1]), parts[0].dtype),
        in_specs=[pl.BlockSpec(memory_space=pltpu.HBM)] * len(parts),
        out_specs=pl.BlockSpec(memory_space=pltpu.VMEM),
        scratch_shapes=[pltpu.SemaphoreType.DMA((len(parts),))],
        compiler_params=pltpu.CompilerParams(vmem_limit_bytes=2**20),
        cost_estimate=pl.CostEstimate(flops=1, bytes_accessed=1, transcendentals=0),
    )(*[pltpu.with_memory_space_constraint(part, pltpu.HBM) for part in parts])


def kernel_call(kernel, outs, flags, *arrays):
    held = [pltpu.with_memory_space_constraint(a, pltpu.VMEM) for a in arrays[-2:]]
    rows = held[0].shape[0] // 2

    def inner(*refs):
        at = len(arrays) - 1
        halves = [ref.at[pl.ds(k * rows, rows)] for ref in refs[at : at + 2] for k in (0, 1)]
        kernel(*refs[:at], *halves, *refs[at + 2 :])

    return pl.pallas_call(
        inner,
        out_shape=[jax.ShapeDtypeStruct(shape, dtype) for shape, dtype in outs],
        in_specs=[pl.BlockSpec(memory_space=pltpu.SMEM)]
        + [pl.BlockSpec(memory_space=pltpu.VMEM)] * len(arrays),
        out_specs=[pl.BlockSpec(memory_space=pltpu.VMEM)] * len(outs),
        compiler_params=pltpu.CompilerParams(vmem_limit_bytes=VMEM_LIMIT),
        cost_estimate=pl.CostEstimate(flops=1, bytes_accessed=1, transcendentals=0),
    )(flags, *arrays[:-2], *held)


def span_dot(weights, low, high, sources):
    totals = [None, None]
    for at in range(0, sources[0].shape[1], SPAN):
        columns = slice(at, at + SPAN)
        left = [ref[low:high, columns] for ref in weights]
        left = left[0] if len(left) == 1 else jnp.concatenate(left)
        for which, source in enumerate(sources):
            part = contract(left, source[:, columns])
            old = totals[which]
            totals[which] = part if old is None else old + part
    return totals


def sums_into(lefts, sources, outs):
    for at in range(0, sources[0].shape[1], SPAN):
        columns = slice(at, at + SPAN)
        part = rows_dot(lefts[0], sources[0][:, columns])
        part = part + rows_dot(lefts[1], sources[1][:, columns])
        row = 0
        for ref in outs:
            rows = ref.shape[0]
            ref[:, columns] = part[row : row + rows].astype(ref.dtype)
            row += rows


def products(flags, flag, weights, tokens, cotangent):
    block = weights[0].shape[0] // 3
    sums = span_dot(weights, 0, 2 * block, tokens)
    backs = span_dot(weights, 2 * block, 3 * block, cotangent)
    found = []
    for which in range(len(weights)):
        pair = []
        row = which * block
        for at in range(2):
            gate_sum = sums[at][2 * row : 2 * row + block]
            up_sum = sums[at][2 * row + block : 2 * row + 2 * block]
            back = backs[at][row : row + block]
            squash = jax.nn.sigmoid(gate_sum)
            activated = gate_sum * squash
            slope = up_sum * squash * (1.0 + gate_sum * (1.0 - squash))
            parts = [back * slope, back * activated, activated * up_sum]
            meets = flags[flag + 2 * which + at] != 0
            pair.append(jnp.where(meets, jnp.concatenate(parts), 0.0).astype(BF16))
        found.append(pair)
    return found


def square(tokens, cotangent, gate_weight, up_weight, down_weight):
    section = lax.axis_index("section")
    core = section % 2
    chip = section // 2
    line = lax.axis_index("dp")
    block = gate_weight.shape[0]
    half = block // 2
    tok, width = tokens.shape
    first = core == 0
    even = chip % 2 == 0
    keep_low = jnp.logical_or(line == 0, line == 3)

    def spread(own):
        v = [(i, i ^ (Y | CORE if i % 4 == 2 else CORE)) for i in range(8)]
        u = [
            (i, i ^ (X | CORE if i % 2 else (Y | CORE if i % 4 == 0 else CORE)))
            for i in range(8)
        ]
        return lax.ppermute(own, "section", v), lax.ppermute(own, "section", u)

    def other(i):
        return Y if i % 2 == 0 else X

    swapped = jnp.logical_and(core == 1, chip % 2 == 1)
    next_chip = jnp.where(first, chip ^ 1, chip ^ 2)
    holders = jnp.stack(
        [
            jnp.where(swapped, next_chip, chip),
            jnp.where(swapped, chip, next_chip),
            jnp.where(first, chip ^ 2, (chip + 3) % 4),
            chip ^ 3,
        ]
    )
    sections = jnp.stack([section, section ^ 1])
    meets = (sections[None, :] - (2 * holders + 1 - core)[:, None]) % 8 < STEPS
    flags = jnp.concatenate(
        [meets.reshape(8).astype(jnp.int32), jnp.stack([first, even]).astype(jnp.int32)]
    )

    low, high = slice(0, 2 * block), slice(2 * block, 3 * block)

    def of_v_u(flags, v, u, t0, t1, c0, c1, found, p_out):
        pairs = products(flags, 0, [v, u], (t0, t1), (c0, c1))
        for which in range(2):
            for at in range(2):
                found[2 * which + at] = pairs[which][at]
        sums_into([part[high] for part in pairs[0]], (c0, c1), [p_out.at[high]])
        sums_into([part[low] for part in pairs[0]], (t0, t1), [p_out.at[low]])

    def of_s(flags, s, t0, t1, c0, c1, gate, up, down):
        (pair,) = products(flags, 4, [s], (t0, t1), (c0, c1))
        sums_into([part[high] for part in pair], (c0, c1), [down])
        sums_into([part[low] for part in pair], (t0, t1), [gate, up])

    def of_e(flags, e, found, t0, t1, c0, c1, *outs):
        (pair,) = products(flags, 6, [e], (t0, t1), (c0, c1))
        leaving, staying = [], []
        for at in range(2):
            v, u = found[at], found[2 + at]
            mixed = jnp.where(flags[8] != 0, pair[at], v)
            leaving.append(jnp.where(flags[9] != 0, mixed, u))
            staying.append(jnp.where(flags[9] != 0, u, mixed))
        for rows, source, some in ((high, (c0, c1), (2, 5)), (low, (t0, t1), (0, 1, 3, 4))):
            lefts = [
                jnp.concatenate([leave[rows], stay[rows]])
                for leave, stay in zip(leaving, staying)
            ]
            sums_into(lefts, source, [outs[at] for at in some])

    narrow, wide = ((block, width), BF16), ((block, width), F32)

    tokens_in = hop(tokens, lambda i: CORE)
    cotangent_in = hop(cotangent, lambda i: CORE)
    own = on_chip(gate_weight, up_weight, down_weight)
    w_v, w_u = spread(own)
    here = [on_chip(tokens, tokens_in), on_chip(cotangent, cotangent_in)]
    w_s = hop(after(w_v, here), other)
    found, p = kernel_call(
        of_v_u,
        [((4, 3 * block, tok), BF16), ((3 * block, width), BF16)],
        flags, w_v, w_u, *here,
    )
    w_e = hop(after(w_u, found), lambda i: Y, 0)
    order = (2, 0, 1)
    p = hop(p, lambda i: X, 0)
    p_in = [p[k * block : (k + 1) * block] for k in range(3)]
    q = kernel_call(of_s, [narrow] * 3, flags, w_s, *here)
    there = {k: hop(q[k], lambda i: X) for k in order[:2]}
    sums = kernel_call(of_e, [wide] * 6, flags, w_e, found, *here)
    there[order[2]] = hop(after(q[order[2]], sums), lambda i: X)
    leave, stay = sums[:3], sums[3:]

    turn = (sums,)
    r, swap, across, back_in = {}, {}, {}, {}
    totals, kept, done, results = {}, {}, {}, {}

    def take(value):
        return after(value, turn)

    def leave_stage(k):
        p_got, q_got = p_in[k], take(there[k])
        out = (leave[k] + jnp.where(even, q_got, p_got).astype(F32)).astype(BF16)
        r[k] = hop(out, lambda i: Y)
        totals[k] = stay[k] + jnp.where(even, p_got, q_got).astype(F32)
        return out

    def swap_stage(k):
        total = totals[k] + take(r[k]).astype(F32)
        upper, lower = total[:half], total[half:]
        out = jnp.where(keep_low, lower, upper).astype(BF16)
        kept[k] = jnp.where(keep_low, upper, lower)
        swap[k] = along(out, PAIRS)
        return out

    def across_stage(k):
        kept[k] = lax.reduce_precision(kept[k] + take(swap[k]).astype(F32), 8, 7)
        out = kept[k].astype(BF16)
        across[k] = along(out, ACROSS)
        return out

    def back_stage(k):
        done[k] = (kept[k] + take(across[k]).astype(F32)).astype(BF16)
        back_in[k] = along(done[k], PAIRS)
        return done[k]

    def result_stage(k):
        mine, got = done[k], take(back_in[k])
        results[k] = jnp.concatenate(
            [jnp.where(keep_low, mine, got), jnp.where(keep_low, got, mine)]
        )
        return results[k]

    stages = [leave_stage, swap_stage, across_stage, back_stage, result_stage]
    steps = [(k, at) for at in range(5) for k in range(3)]
    for k, at in steps:
        turn = stages[at](order[k])
    return results[0], results[1], results[2]


def solution(mesh):
    fits = mesh.shape["section"] == 8 and mesh.shape["dp"] == 4
    return jax.shard_map(
        square if fits else ring,
        mesh=mesh,
        in_specs=(
            P(("section", "dp"), None),
            P(("section", "dp"), None),
            P("section", None),
            P("section", None),
            P("section", None),
        ),
        out_specs=(P("section", None), P("section", None), P("section", None)),
        check_vma=False,
    )
```

```python
import jax
import jax.numpy as jnp
from jax import lax
from jax.experimental import pallas as pl
from jax.experimental.pallas import tpu as pltpu
from jax.sharding import PartitionSpec as P

STEPS = 6
F32 = jnp.float32
BF16 = jnp.bfloat16


def from_behind(block, axis, distance):
    devices = range(lax.axis_size(axis))
    route = [((i - distance) % len(devices), i) for i in devices]
    return lax.ppermute(block, axis, route)


def contract(left, right):
    return lax.dot_general(
        left, right, (((1,), (1,)), ((), ())), preferred_element_type=F32
    )


def rows_dot(left, right):
    return jnp.dot(left, right, preferred_element_type=F32)


def activations(tokens, cotangent, gate, upper, down):
    gate_sum = contract(gate, tokens)
    up_sum = contract(upper, tokens)
    squash = jax.nn.sigmoid(gate_sum)
    activated = gate_sum * squash
    hidden = (activated * up_sum).astype(BF16)
    backward = contract(down, cotangent)
    gate_back = (backward * up_sum * squash * (1.0 + gate_sum * (1.0 - squash))).astype(
        BF16
    )
    up_back = (backward * activated).astype(BF16)
    return gate_back, up_back, hidden


def ring(tokens, cotangent, gate_weight, up_weight, down_weight):
    held = jnp.stack([gate_weight, up_weight, down_weight])
    summed = None
    for position in range(STEPS):
        if position > 0:
            held = from_behind(held, "section", 1)
        parts = activations(tokens, cotangent, held[0], held[1], held[2])
        piece = jnp.stack(
            [
                rows_dot(parts[0], tokens),
                rows_dot(parts[1], tokens),
                rows_dot(parts[2], cotangent),
            ]
        )
        if position > 0:
            summed = from_behind(summed, "section", 1) + piece
        else:
            summed = piece
    finished = lax.psum(summed, "dp").astype(BF16)
    return (finished[0], finished[1], finished[2])


def hop(block, step, only=None):
    route = [(i, i ^ step(i)) for i in range(8) if only is None or i % 2 == only]
    return lax.ppermute(block, "section", route)


def along(block, route):
    return lax.ppermute(block, "dp", route)


CORE, X, Y = 1, 2, 4
PAIRS = [(0, 1), (1, 0), (2, 3), (3, 2)]
ACROSS = [(0, 3), (3, 0), (1, 2), (2, 1)]
SPAN = 512
VMEM_LIMIT = 8 * 2**20


def after(value, *others):
    return lax.optimization_barrier((value, others))[0]


def on_chip(*parts):
    def kernel(*refs):
        sources, out, sems = refs[: len(parts)], refs[-2], refs[-1]
        copies, row = [], 0
        for at, source in enumerate(sources):
            rows = source.shape[0]
            spot = out.at[pl.ds(row, rows)]
            copies.append(pltpu.make_async_copy(source, spot, sems.at[at]))
            row += rows
        for copy in copies:
            copy.start()
        for copy in copies:
            copy.wait()

    rows = sum(part.shape[0] for part in parts)
    return pl.pallas_call(
        kernel,
        out_shape=pltpu.VMEM((rows, parts[0].shape[1]), parts[0].dtype),
        in_specs=[pl.BlockSpec(memory_space=pltpu.HBM)] * len(parts),
        out_specs=pl.BlockSpec(memory_space=pltpu.VMEM),
        scratch_shapes=[pltpu.SemaphoreType.DMA((len(parts),))],
        compiler_params=pltpu.CompilerParams(vmem_limit_bytes=2**20),
        cost_estimate=pl.CostEstimate(flops=1, bytes_accessed=1, transcendentals=0),
    )(*[pltpu.with_memory_space_constraint(part, pltpu.HBM) for part in parts])


def kernel_call(kernel, outs, flags, *arrays):
    held = [pltpu.with_memory_space_constraint(a, pltpu.VMEM) for a in arrays[-2:]]
    rows = held[0].shape[0] // 2

    def inner(*refs):
        at = len(arrays) - 1
        halves = [ref.at[pl.ds(k * rows, rows)] for ref in refs[at : at + 2] for k in (0, 1)]
        kernel(*refs[:at], *halves, *refs[at + 2 :])

    return pl.pallas_call(
        inner,
        out_shape=[jax.ShapeDtypeStruct(shape, dtype) for shape, dtype in outs],
        in_specs=[pl.BlockSpec(memory_space=pltpu.SMEM)]
        + [pl.BlockSpec(memory_space=pltpu.VMEM)] * len(arrays),
        out_specs=[pl.BlockSpec(memory_space=pltpu.VMEM)] * len(outs),
        compiler_params=pltpu.CompilerParams(vmem_limit_bytes=VMEM_LIMIT),
        cost_estimate=pl.CostEstimate(flops=1, bytes_accessed=8388608, transcendentals=0),
    )(flags, *arrays[:-2], *held)


def span_dot(weights, low, high, sources):
    totals = [None] * len(sources)
    for at in range(0, sources[0].shape[1], SPAN):
        columns = slice(at, at + SPAN)
        left = [ref[low:high, columns] for ref in weights]
        left = left[0] if len(left) == 1 else jnp.concatenate(left)
        for which, source in enumerate(sources):
            part = contract(left, source[:, columns])
            old = totals[which]
            totals[which] = part if old is None else old + part
    return totals


def sums_into(lefts, sources, outs):
    for at in range(0, sources[0].shape[1], SPAN):
        columns = slice(at, at + SPAN)
        part = None
        for left, source in zip(lefts, sources):
            one = rows_dot(left, source[:, columns])
            part = one if part is None else part + one
        row = 0
        for ref in outs:
            rows = ref.shape[0]
            ref[:, columns] = part[row : row + rows].astype(ref.dtype)
            row += rows


def products(flags, flag, weights, tokens, cotangent):
    block = weights[0].shape[0] // 3
    sums = span_dot(weights, 0, 2 * block, tokens)
    backs = span_dot(weights, 2 * block, 3 * block, cotangent)
    found = []
    for which in range(len(weights)):
        pair = []
        row = which * block
        for at in range(len(tokens)):
            gate_sum = sums[at][2 * row : 2 * row + block]
            up_sum = sums[at][2 * row + block : 2 * row + 2 * block]
            back = backs[at][row : row + block]
            squash = jax.nn.sigmoid(gate_sum)
            activated = gate_sum * squash
            slope = up_sum * squash * (1.0 + gate_sum * (1.0 - squash))
            parts = [back * slope, back * activated, activated * up_sum]
            part = jnp.concatenate(parts)
            if flag is not None:
                part = jnp.where(flags[flag + 2 * which + at] != 0, part, 0.0)
            pair.append(part.astype(BF16))
        found.append(pair)
    return found


def square(tokens, cotangent, gate_weight, up_weight, down_weight):
    section = lax.axis_index("section")
    core = section % 2
    chip = section // 2
    line = lax.axis_index("dp")
    block = gate_weight.shape[0]
    half = block // 2
    tok, width = tokens.shape
    first = core == 0
    even = chip % 2 == 0
    keep_low = jnp.logical_or(line == 0, line == 3)

    def spread(own):
        v = [(i, i ^ (Y | CORE if i % 4 == 2 else CORE)) for i in range(8)]
        u = [
            (i, i ^ (X | CORE if i % 2 else (Y | CORE if i % 4 == 0 else CORE)))
            for i in range(8)
        ]
        return lax.ppermute(own, "section", v), lax.ppermute(own, "section", u)

    def other(i):
        return Y if i % 2 == 0 else X

    swapped = jnp.logical_and(core == 1, chip % 2 == 1)
    next_chip = jnp.where(first, chip ^ 1, chip ^ 2)
    holders = jnp.stack(
        [
            jnp.where(swapped, next_chip, chip),
            jnp.where(swapped, chip, next_chip),
            jnp.where(first, chip ^ 2, (chip + 3) % 4),
            chip ^ 3,
        ]
    )
    sections = jnp.stack([section, section ^ 1])
    meets = (sections[None, :] - (2 * holders + 1 - core)[:, None]) % 8 < STEPS
    flags = jnp.concatenate(
        [meets.reshape(8).astype(jnp.int32), jnp.stack([first, even]).astype(jnp.int32)]
    )

    low, high = slice(0, 2 * block), slice(2 * block, 3 * block)

    def of_pair(flags, own, t0, t1, c0, c1, p_out):
        (pair,) = products(flags, None, [own], (t1,), (c1,))
        sums_into([pair[0][high]], (c1,), [p_out.at[high]])
        sums_into([pair[0][low]], (t1,), [p_out.at[low]])

    def of_v_u(flags, v, u, t0, t1, c0, c1, found):
        pairs = products(flags, 0, [v, u], (t0, t1), (c0, c1))
        for which in range(2):
            for at in range(2):
                found[2 * which + at] = pairs[which][at]

    def of_s(flags, s, t0, t1, c0, c1, gate, up, down):
        (pair,) = products(flags, 4, [s], (t0, t1), (c0, c1))
        sums_into([part[high] for part in pair], (c0, c1), [down])
        sums_into([part[low] for part in pair], (t0, t1), [gate, up])

    def of_e(flags, e, found, t0, t1, c0, c1, *outs):
        (pair,) = products(flags, 6, [e], (t0, t1), (c0, c1))
        leaving, staying = [], []
        for at in range(2):
            v, u = found[at], found[2 + at]
            mixed = jnp.where(flags[8] != 0, pair[at], v)
            leaving.append(jnp.where(flags[9] != 0, mixed, u))
            staying.append(jnp.where(flags[9] != 0, u, mixed))
        for rows, source, some in ((high, (c0, c1), (2, 5)), (low, (t0, t1), (0, 1, 3, 4))):
            lefts = [
                jnp.concatenate([leave[rows], stay[rows]])
                for leave, stay in zip(leaving, staying)
            ]
            sums_into(lefts, source, [outs[at] for at in some])

    narrow, wide = ((block, width), BF16), ((block, width), F32)

    tokens_in = hop(tokens, lambda i: CORE)
    cotangent_in = hop(cotangent, lambda i: CORE)
    own = on_chip(gate_weight, up_weight, down_weight)
    w_p = hop(own, lambda i: CORE)
    w_v, w_u = spread(own)
    here = [on_chip(tokens, tokens_in), on_chip(cotangent, cotangent_in)]
    (p,) = kernel_call(of_pair, [((3 * block, width), BF16)], flags, w_p, *here)
    w_s = hop(after(w_v, p), other)
    p = hop(p, lambda i: X, 0)
    (found,) = kernel_call(
        of_v_u, [((4, 3 * block, tok), BF16)], flags, w_v, w_u, *here
    )
    w_e = hop(after(w_u, found), lambda i: Y, 0)
    order = (2, 0, 1)
    p_in = [p[k * block : (k + 1) * block] for k in range(3)]
    q = kernel_call(of_s, [narrow] * 3, flags, w_s, *here)
    there = {k: hop(q[k], lambda i: X) for k in order[:2]}
    sums = kernel_call(of_e, [wide] * 6, flags, w_e, found, *here)
    there[order[2]] = hop(q[order[2]], lambda i: X)
    leave, stay = sums[:3], sums[3:]

    turn = (sums,)
    r, swap, across, back_in = {}, {}, {}, {}
    totals, kept, done, results = {}, {}, {}, {}

    def take(value):
        return after(value, turn)

    def leave_stage(k):
        p_got, q_got = p_in[k], take(there[k])
        out = (leave[k] + jnp.where(even, q_got, p_got).astype(F32)).astype(BF16)
        r[k] = hop(out, lambda i: Y)
        totals[k] = stay[k] + jnp.where(even, p_got, q_got).astype(F32)
        totals[k] = lax.optimization_barrier(totals[k])
        return out

    def swap_stage(k):
        total = totals[k] + take(r[k]).astype(F32)
        upper, lower = total[:half], total[half:]
        out = jnp.where(keep_low, lower, upper).astype(BF16)
        kept[k] = jnp.where(keep_low, upper, lower)
        swap[k] = along(out, PAIRS)
        return out

    def across_stage(k):
        kept[k] = lax.reduce_precision(kept[k] + take(swap[k]).astype(F32), 8, 7)
        out = kept[k].astype(BF16)
        across[k] = along(out, ACROSS)
        return out

    def back_stage(k):
        done[k] = (kept[k] + take(across[k]).astype(F32)).astype(BF16)
        back_in[k] = along(done[k], PAIRS)
        return done[k]

    def result_stage(k):
        mine, got = done[k], take(back_in[k])
        results[k] = jnp.concatenate(
            [jnp.where(keep_low, mine, got), jnp.where(keep_low, got, mine)]
        )
        return results[k]

    stages = [leave_stage, swap_stage, across_stage, back_stage, result_stage]
    steps = ((0, 0), (1, 0), (0, 1), (2, 0), (1, 1), (0, 2), (2, 1), (1, 2), (2, 2), (0, 3), (1, 3), (2, 3), (0, 4), (1, 4), (2, 4))
    for k, at in steps:
        turn = stages[at](order[k])
    return results[0], results[1], results[2]


def solution(mesh):
    fits = mesh.shape["section"] == 8 and mesh.shape["dp"] == 4
    return jax.shard_map(
        square if fits else ring,
        mesh=mesh,
        in_specs=(
            P(("section", "dp"), None),
            P(("section", "dp"), None),
            P("section", None),
            P("section", None),
            P("section", None),
        ),
        out_specs=(P("section", None), P("section", None), P("section", None)),
        check_vma=False,
    )
```

```python
import jax
import jax.numpy as jnp
from jax import lax
from jax.experimental import pallas as pl
from jax.experimental.pallas import tpu as pltpu
from jax.sharding import PartitionSpec as P

STEPS = 6
F32 = jnp.float32
BF16 = jnp.bfloat16


def from_behind(block, axis, distance):
    devices = range(lax.axis_size(axis))
    route = [((i - distance) % len(devices), i) for i in devices]
    return lax.ppermute(block, axis, route)


def contract(left, right):
    return lax.dot_general(
        left, right, (((1,), (1,)), ((), ())), preferred_element_type=F32
    )


def rows_dot(left, right):
    return jnp.dot(left, right, preferred_element_type=F32)


def activations(tokens, cotangent, gate, upper, down):
    gate_sum = contract(gate, tokens)
    up_sum = contract(upper, tokens)
    squash = jax.nn.sigmoid(gate_sum)
    activated = gate_sum * squash
    hidden = (activated * up_sum).astype(BF16)
    backward = contract(down, cotangent)
    gate_back = (backward * up_sum * squash * (1.0 + gate_sum * (1.0 - squash))).astype(
        BF16
    )
    up_back = (backward * activated).astype(BF16)
    return gate_back, up_back, hidden


def ring(tokens, cotangent, gate_weight, up_weight, down_weight):
    held = jnp.stack([gate_weight, up_weight, down_weight])
    summed = None
    for position in range(STEPS):
        if position > 0:
            held = from_behind(held, "section", 1)
        parts = activations(tokens, cotangent, held[0], held[1], held[2])
        piece = jnp.stack(
            [
                rows_dot(parts[0], tokens),
                rows_dot(parts[1], tokens),
                rows_dot(parts[2], cotangent),
            ]
        )
        if position > 0:
            summed = from_behind(summed, "section", 1) + piece
        else:
            summed = piece
    finished = lax.psum(summed, "dp").astype(BF16)
    return (finished[0], finished[1], finished[2])


def hop(block, step, only=None):
    route = [(i, i ^ step(i)) for i in range(8) if only is None or i % 2 == only]
    return lax.ppermute(block, "section", route)


def along(block, route):
    return lax.ppermute(block, "dp", route)


CORE, X, Y = 1, 2, 4
PAIRS = [(0, 1), (1, 0), (2, 3), (3, 2)]
ACROSS = [(0, 3), (3, 0), (1, 2), (2, 1)]
SPAN = 512
VMEM_LIMIT = 8 * 2**20


def after(value, *others):
    return lax.optimization_barrier((value, others))[0]


def on_chip(*parts):
    def kernel(*refs):
        sources, out, sems = refs[: len(parts)], refs[-2], refs[-1]
        copies, row = [], 0
        for at, source in enumerate(sources):
            rows = source.shape[0]
            spot = out.at[pl.ds(row, rows)]
            copies.append(pltpu.make_async_copy(source, spot, sems.at[at]))
            row += rows
        for copy in copies:
            copy.start()
        for copy in copies:
            copy.wait()

    rows = sum(part.shape[0] for part in parts)
    return pl.pallas_call(
        kernel,
        out_shape=pltpu.VMEM((rows, parts[0].shape[1]), parts[0].dtype),
        in_specs=[pl.BlockSpec(memory_space=pltpu.HBM)] * len(parts),
        out_specs=pl.BlockSpec(memory_space=pltpu.VMEM),
        scratch_shapes=[pltpu.SemaphoreType.DMA((len(parts),))],
        compiler_params=pltpu.CompilerParams(vmem_limit_bytes=2**20),
        cost_estimate=pl.CostEstimate(flops=1, bytes_accessed=1, transcendentals=0),
    )(*[pltpu.with_memory_space_constraint(part, pltpu.HBM) for part in parts])


def kernel_call(kernel, outs, flags, *arrays):
    held = pltpu.with_memory_space_constraint(arrays[-1], pltpu.VMEM)
    rows = held.shape[0] // 4
    width, sent = held.shape[1], pltpu.HBM

    def inner(*refs):
        at = len(arrays)
        parts = [refs[at].at[pl.ds(k * rows, rows)] for k in range(4)]
        kernel(*refs[:at], *parts, *refs[at + 1 :])

    return pl.pallas_call(
        inner,
        out_shape=[
            sent(shape, dtype)
            if shape[-1] == width and dtype == BF16
            else jax.ShapeDtypeStruct(shape, dtype)
            for shape, dtype in outs
        ],
        in_specs=[pl.BlockSpec(memory_space=pltpu.SMEM)]
        + [pl.BlockSpec(memory_space=pltpu.VMEM)] * len(arrays),
        out_specs=[pl.BlockSpec(memory_space=pltpu.VMEM)] * len(outs),
        compiler_params=pltpu.CompilerParams(vmem_limit_bytes=VMEM_LIMIT),
        cost_estimate=pl.CostEstimate(flops=1, bytes_accessed=8388608, transcendentals=0),
    )(flags, *arrays[:-1], held)


def span_dot(weights, low, high, sources):
    totals = [None] * len(sources)
    for at in range(0, sources[0].shape[1], SPAN):
        columns = slice(at, at + SPAN)
        left = [ref[low:high, columns] for ref in weights]
        left = left[0] if len(left) == 1 else jnp.concatenate(left)
        for which, source in enumerate(sources):
            part = contract(left, source[:, columns])
            old = totals[which]
            totals[which] = part if old is None else old + part
    return totals


def sums_into(lefts, sources, outs):
    for at in range(0, sources[0].shape[1], SPAN):
        columns = slice(at, at + SPAN)
        part = None
        for left, source in zip(lefts, sources):
            one = rows_dot(left, source[:, columns])
            part = one if part is None else part + one
        row = 0
        for ref in outs:
            rows = ref.shape[0]
            ref[:, columns] = part[row : row + rows].astype(ref.dtype)
            row += rows


def products(flags, flag, weights, tokens, cotangent):
    block = weights[0].shape[0] // 3
    sums = span_dot(weights, 0, 2 * block, tokens)
    backs = span_dot(weights, 2 * block, 3 * block, cotangent)
    found = []
    for which in range(len(weights)):
        pair = []
        row = which * block
        for at in range(len(tokens)):
            gate_sum = sums[at][2 * row : 2 * row + block]
            up_sum = sums[at][2 * row + block : 2 * row + 2 * block]
            back = backs[at][row : row + block]
            squash = jax.nn.sigmoid(gate_sum)
            activated = gate_sum * squash
            slope = up_sum * squash * (1.0 + gate_sum * (1.0 - squash))
            parts = [back * slope, back * activated, activated * up_sum]
            part = jnp.concatenate(parts)
            if flag is not None:
                part = jnp.where(flags[flag + 2 * which + at] != 0, part, 0.0)
            pair.append(part.astype(BF16))
        found.append(pair)
    return found


def square(tokens, cotangent, gate_weight, up_weight, down_weight):
    section = lax.axis_index("section")
    core = section % 2
    chip = section // 2
    line = lax.axis_index("dp")
    block = gate_weight.shape[0]
    half = block // 2
    tok, width = tokens.shape
    first = core == 0
    even = chip % 2 == 0
    keep_low = jnp.logical_or(line == 0, line == 3)

    def spread(own):
        v = [(i, i ^ (Y | CORE if i % 4 == 2 else CORE)) for i in range(8)]
        u = [
            (i, i ^ (X | CORE if i % 2 else (Y | CORE if i % 4 == 0 else CORE)))
            for i in range(8)
        ]
        return lax.ppermute(own, "section", v), lax.ppermute(own, "section", u)

    def other(i):
        return Y if i % 2 == 0 else X

    swapped = jnp.logical_and(core == 1, chip % 2 == 1)
    next_chip = jnp.where(first, chip ^ 1, chip ^ 2)
    holders = jnp.stack(
        [
            jnp.where(swapped, next_chip, chip),
            jnp.where(swapped, chip, next_chip),
            jnp.where(first, chip ^ 2, (chip + 3) % 4),
            chip ^ 3,
        ]
    )
    sections = jnp.stack([section, section ^ 1])
    meets = (sections[None, :] - (2 * holders + 1 - core)[:, None]) % 8 < STEPS
    flags = jnp.concatenate(
        [meets.reshape(8).astype(jnp.int32), jnp.stack([first, even]).astype(jnp.int32)]
    )

    low, high = slice(0, 2 * block), slice(2 * block, 3 * block)

    def of_pair(flags, own, t0, t1, c0, c1, p_out):
        (pair,) = products(flags, None, [own], (t1,), (c1,))
        sums_into([pair[0][high]], (c1,), [p_out.at[high]])
        sums_into([pair[0][low]], (t1,), [p_out.at[low]])

    def of_v_u(flags, v, u, t0, t1, c0, c1, found):
        pairs = products(flags, 0, [v, u], (t0, t1), (c0, c1))
        for which in range(2):
            for at in range(2):
                found[2 * which + at] = pairs[which][at]

    def of_s(flags, s, t0, t1, c0, c1, gate, up, down):
        (pair,) = products(flags, 4, [s], (t0, t1), (c0, c1))
        sums_into([part[high] for part in pair], (c0, c1), [down])
        sums_into([part[low] for part in pair], (t0, t1), [gate, up])

    def of_e(flags, e, found, t0, t1, c0, c1, *outs):
        (pair,) = products(flags, 6, [e], (t0, t1), (c0, c1))
        leaving, staying = [], []
        for at in range(2):
            v, u = found[at], found[2 + at]
            mixed = jnp.where(flags[8] != 0, pair[at], v)
            leaving.append(jnp.where(flags[9] != 0, mixed, u))
            staying.append(jnp.where(flags[9] != 0, u, mixed))
        for rows, source, some in ((high, (c0, c1), (2, 5)), (low, (t0, t1), (0, 1, 3, 4))):
            lefts = [
                jnp.concatenate([leave[rows], stay[rows]])
                for leave, stay in zip(leaving, staying)
            ]
            sums_into(lefts, source, [outs[at] for at in some])

    narrow, wide = ((block, width), BF16), ((block, width), F32)

    tokens_in = hop(tokens, lambda i: CORE)
    cotangent_in = hop(cotangent, lambda i: CORE)
    own = on_chip(gate_weight, up_weight, down_weight)
    w_p = hop(own, lambda i: CORE)
    w_v, w_u = spread(own)
    here = [on_chip(tokens, tokens_in, cotangent, cotangent_in)]
    (p,) = kernel_call(of_pair, [((3 * block, width), BF16)], flags, w_p, *here)
    w_s = hop(after(w_v, p), other)
    p = hop(p, lambda i: X, 0)
    (found,) = kernel_call(
        of_v_u, [((4, 3 * block, tok), BF16)], flags, w_v, w_u, *here
    )
    w_e = hop(after(w_u, found), lambda i: Y, 0)
    order = (2, 0, 1)
    p_in = [p[k * block : (k + 1) * block] for k in range(3)]
    q = kernel_call(of_s, [narrow] * 3, flags, w_s, *here)
    there = {k: hop(q[k], lambda i: X) for k in order[:2]}
    sums = kernel_call(of_e, [wide] * 6, flags, w_e, found, *here)
    there[order[2]] = hop(q[order[2]], lambda i: X)
    leave, stay = sums[:3], sums[3:]

    turn = (sums,)
    r, swap, across, back_in = {}, {}, {}, {}
    totals, kept, done, results = {}, {}, {}, {}

    def take(value):
        return after(value, turn)

    def leave_stage(k):
        p_got, q_got = p_in[k], take(there[k])
        out = (leave[k] + jnp.where(even, q_got, p_got).astype(F32)).astype(BF16)
        r[k] = hop(out, lambda i: Y)
        totals[k] = stay[k] + jnp.where(even, p_got, q_got).astype(F32)
        totals[k] = lax.optimization_barrier(totals[k])
        return out

    def swap_stage(k):
        total = totals[k] + take(r[k]).astype(F32)
        upper, lower = total[:half], total[half:]
        out = jnp.where(keep_low, lower, upper).astype(BF16)
        kept[k] = jnp.where(keep_low, upper, lower)
        swap[k] = along(out, PAIRS)
        return out

    def across_stage(k):
        kept[k] = lax.reduce_precision(kept[k] + take(swap[k]).astype(F32), 8, 7)
        out = kept[k].astype(BF16)
        across[k] = along(out, ACROSS)
        return out

    def back_stage(k):
        done[k] = (kept[k] + take(across[k]).astype(F32)).astype(BF16)
        back_in[k] = along(done[k], PAIRS)
        return done[k]

    def result_stage(k):
        mine, got = done[k], take(back_in[k])
        results[k] = jnp.concatenate(
            [jnp.where(keep_low, mine, got), jnp.where(keep_low, got, mine)]
        )
        return results[k]

    stages = [leave_stage, swap_stage, across_stage, back_stage, result_stage]
    steps = ((0, 0), (1, 0), (0, 1), (2, 0), (1, 1), (0, 2), (2, 1), (1, 2), (2, 2), (0, 3), (1, 3), (2, 3), (1, 4), (0, 4), (2, 4))
    for k, at in steps:
        turn = stages[at](order[k])
    return results[0], results[1], results[2]


def solution(mesh):
    fits = mesh.shape["section"] == 8 and mesh.shape["dp"] == 4
    return jax.shard_map(
        square if fits else ring,
        mesh=mesh,
        in_specs=(
            P(("section", "dp"), None),
            P(("section", "dp"), None),
            P("section", None),
            P("section", None),
            P("section", None),
        ),
        out_specs=(P("section", None), P("section", None), P("section", None)),
        check_vma=False,
    )
```

```python
import jax
import jax.numpy as jnp
from jax import lax
from jax.experimental import pallas as pl
from jax.experimental.pallas import tpu as pltpu
from jax.sharding import PartitionSpec as P

STEPS = 6
F32 = jnp.float32
BF16 = jnp.bfloat16


def from_behind(block, axis, distance):
    devices = range(lax.axis_size(axis))
    route = [((i - distance) % len(devices), i) for i in devices]
    return lax.ppermute(block, axis, route)


def contract(left, right):
    return lax.dot_general(
        left, right, (((1,), (1,)), ((), ())), preferred_element_type=F32
    )


def rows_dot(left, right):
    return jnp.dot(left, right, preferred_element_type=F32)


def activations(tokens, cotangent, gate, upper, down):
    gate_sum = contract(gate, tokens)
    up_sum = contract(upper, tokens)
    squash = jax.nn.sigmoid(gate_sum)
    activated = gate_sum * squash
    hidden = (activated * up_sum).astype(BF16)
    backward = contract(down, cotangent)
    gate_back = (backward * up_sum * squash * (1.0 + gate_sum * (1.0 - squash))).astype(
        BF16
    )
    up_back = (backward * activated).astype(BF16)
    return gate_back, up_back, hidden


def ring(tokens, cotangent, gate_weight, up_weight, down_weight):
    held = jnp.stack([gate_weight, up_weight, down_weight])
    summed = None
    for position in range(STEPS):
        if position > 0:
            held = from_behind(held, "section", 1)
        parts = activations(tokens, cotangent, held[0], held[1], held[2])
        piece = jnp.stack(
            [
                rows_dot(parts[0], tokens),
                rows_dot(parts[1], tokens),
                rows_dot(parts[2], cotangent),
            ]
        )
        if position > 0:
            summed = from_behind(summed, "section", 1) + piece
        else:
            summed = piece
    finished = lax.psum(summed, "dp").astype(BF16)
    return (finished[0], finished[1], finished[2])


def hop(block, step, only=None):
    route = [(i, i ^ step(i)) for i in range(8) if only is None or i % 2 == only]
    return lax.ppermute(block, "section", route)


def along(block, route):
    return lax.ppermute(block, "dp", route)


CORE, X, Y = 1, 2, 4
PAIRS = [(0, 1), (1, 0), (2, 3), (3, 2)]
ACROSS = [(0, 3), (3, 0), (1, 2), (2, 1)]
SPAN = 1024
VMEM_LIMIT = 8 * 2**20


def after(value, *others):
    return lax.optimization_barrier((value, others))[0]


def on_chip(*parts):
    def kernel(*refs):
        sources, out, sems = refs[: len(parts)], refs[-2], refs[-1]
        copies, row = [], 0
        for at, source in enumerate(sources):
            rows = source.shape[0]
            spot = out.at[pl.ds(row, rows)]
            copies.append(pltpu.make_async_copy(source, spot, sems.at[at]))
            row += rows
        for copy in copies:
            copy.start()
        for copy in copies:
            copy.wait()

    rows = sum(part.shape[0] for part in parts)
    return pl.pallas_call(
        kernel,
        out_shape=pltpu.VMEM((rows, parts[0].shape[1]), parts[0].dtype),
        in_specs=[pl.BlockSpec(memory_space=pltpu.HBM)] * len(parts),
        out_specs=pl.BlockSpec(memory_space=pltpu.VMEM),
        scratch_shapes=[pltpu.SemaphoreType.DMA((len(parts),))],
        compiler_params=pltpu.CompilerParams(vmem_limit_bytes=2**20),
        cost_estimate=pl.CostEstimate(flops=1, bytes_accessed=1, transcendentals=0),
    )(*[pltpu.with_memory_space_constraint(part, pltpu.HBM) for part in parts])


def kernel_call(kernel, outs, flags, *arrays):
    held = pltpu.with_memory_space_constraint(arrays[-1], pltpu.VMEM)
    rows = held.shape[0] // 4
    width, sent = held.shape[1], pltpu.HBM

    def inner(*refs):
        at = len(arrays)
        parts = [refs[at].at[pl.ds(k * rows, rows)] for k in range(4)]
        kernel(*refs[:at], *parts, *refs[at + 1 :])

    return pl.pallas_call(
        inner,
        out_shape=[
            sent(shape, dtype)
            if shape[-1] == width and dtype == BF16
            else jax.ShapeDtypeStruct(shape, dtype)
            for shape, dtype in outs
        ],
        in_specs=[pl.BlockSpec(memory_space=pltpu.SMEM)]
        + [pl.BlockSpec(memory_space=pltpu.VMEM)] * len(arrays),
        out_specs=[pl.BlockSpec(memory_space=pltpu.VMEM)] * len(outs),
        compiler_params=pltpu.CompilerParams(vmem_limit_bytes=VMEM_LIMIT),
        cost_estimate=pl.CostEstimate(flops=1, bytes_accessed=8388608, transcendentals=0),
    )(flags, *arrays[:-1], held)


def span_dot(weights, low, high, sources):
    totals = [None] * len(sources)
    for at in range(0, sources[0].shape[1], SPAN):
        columns = slice(at, at + SPAN)
        left = [ref[low:high, columns] for ref in weights]
        left = left[0] if len(left) == 1 else jnp.concatenate(left)
        for which, source in enumerate(sources):
            part = contract(source[:, columns], left)
            old = totals[which]
            totals[which] = part if old is None else old + part
    return [total.T for total in totals]


def sums_into(lefts, sources, outs):
    for at in range(0, sources[0].shape[1], SPAN):
        columns = slice(at, at + SPAN)
        part = None
        for left, source in zip(lefts, sources):
            one = rows_dot(left, source[:, columns])
            part = one if part is None else part + one
        row = 0
        for ref in outs:
            rows = ref.shape[0]
            ref[:, columns] = part[row : row + rows].astype(ref.dtype)
            row += rows


def products(flags, flag, weights, tokens, cotangent):
    block = weights[0].shape[0] // 3
    sums = span_dot(weights, 0, 2 * block, tokens)
    backs = span_dot(weights, 2 * block, 3 * block, cotangent)
    found = []
    for which in range(len(weights)):
        pair = []
        row = which * block
        for at in range(len(tokens)):
            gate_sum = sums[at][2 * row : 2 * row + block]
            up_sum = sums[at][2 * row + block : 2 * row + 2 * block]
            back = backs[at][row : row + block]
            squash = jax.nn.sigmoid(gate_sum)
            activated = gate_sum * squash
            slope = up_sum * squash * (1.0 + gate_sum * (1.0 - squash))
            parts = [back * slope, back * activated, activated * up_sum]
            part = jnp.concatenate(parts)
            if flag is not None:
                part = jnp.where(flags[flag + 2 * which + at] != 0, part, 0.0)
            pair.append(part.astype(BF16))
        found.append(pair)
    return found


def square(tokens, cotangent, gate_weight, up_weight, down_weight):
    section = lax.axis_index("section")
    core = section % 2
    chip = section // 2
    line = lax.axis_index("dp")
    block = gate_weight.shape[0]
    half = block // 2
    tok, width = tokens.shape
    first = core == 0
    even = chip % 2 == 0
    keep_low = jnp.logical_or(line == 0, line == 3)

    def spread(own):
        v = [(i, i ^ (Y | CORE if i % 4 == 2 else CORE)) for i in range(8)]
        u = [
            (i, i ^ (X | CORE if i % 2 else (Y | CORE if i % 4 == 0 else CORE)))
            for i in range(8)
        ]
        return lax.ppermute(own, "section", v), lax.ppermute(own, "section", u)

    def other(i):
        return Y if i % 2 == 0 else X

    swapped = jnp.logical_and(core == 1, chip % 2 == 1)
    next_chip = jnp.where(first, chip ^ 1, chip ^ 2)
    holders = jnp.stack(
        [
            jnp.where(swapped, next_chip, chip),
            jnp.where(swapped, chip, next_chip),
            jnp.where(first, chip ^ 2, (chip + 3) % 4),
            chip ^ 3,
        ]
    )
    sections = jnp.stack([section, section ^ 1])
    meets = (sections[None, :] - (2 * holders + 1 - core)[:, None]) % 8 < STEPS
    flags = jnp.concatenate(
        [meets.reshape(8).astype(jnp.int32), jnp.stack([first, even]).astype(jnp.int32)]
    )

    low, high = slice(0, 2 * block), slice(2 * block, 3 * block)

    def of_pair(flags, own, t0, t1, c0, c1, p_out):
        (pair,) = products(flags, None, [own], (t1,), (c1,))
        sums_into([pair[0][high]], (c1,), [p_out.at[high]])
        sums_into([pair[0][low]], (t1,), [p_out.at[low]])

    def of_v_u(flags, v, u, t0, t1, c0, c1, found):
        pairs = products(flags, 0, [v, u], (t0, t1), (c0, c1))
        for which in range(2):
            for at in range(2):
                found[2 * which + at] = pairs[which][at]

    def of_s(flags, s, t0, t1, c0, c1, gate, up, down):
        (pair,) = products(flags, 4, [s], (t0, t1), (c0, c1))
        sums_into([part[high] for part in pair], (c0, c1), [down])
        sums_into([part[low] for part in pair], (t0, t1), [gate, up])

    def of_e(flags, e, found, t0, t1, c0, c1, *outs):
        (pair,) = products(flags, 6, [e], (t0, t1), (c0, c1))
        leaving, staying = [], []
        for at in range(2):
            v, u = found[at], found[2 + at]
            mixed = jnp.where(flags[8] != 0, pair[at], v)
            leaving.append(jnp.where(flags[9] != 0, mixed, u))
            staying.append(jnp.where(flags[9] != 0, u, mixed))
        for rows, source, some in ((high, (c0, c1), (2, 5)), (low, (t0, t1), (0, 1, 3, 4))):
            lefts = [
                jnp.concatenate([leave[rows], stay[rows]])
                for leave, stay in zip(leaving, staying)
            ]
            sums_into(lefts, source, [outs[at] for at in some])

    narrow, wide = ((block, width), BF16), ((block, width), F32)

    tokens_in = hop(tokens, lambda i: CORE)
    cotangent_in = hop(cotangent, lambda i: CORE)
    own = on_chip(gate_weight, up_weight, down_weight)
    w_p = hop(own, lambda i: CORE)
    w_v, w_u = spread(own)
    here = [on_chip(tokens, tokens_in, cotangent, cotangent_in)]
    (p,) = kernel_call(of_pair, [((3 * block, width), BF16)], flags, w_p, *here)
    w_s = hop(after(w_v, p), other)
    p = hop(p, lambda i: X, 0)
    (found,) = kernel_call(
        of_v_u, [((4, 3 * block, tok), BF16)], flags, w_v, w_u, *here
    )
    w_e = hop(after(w_u, found), lambda i: Y, 0)
    order = (2, 0, 1)
    p_in = [p[k * block : (k + 1) * block] for k in range(3)]
    q = kernel_call(of_s, [narrow] * 3, flags, w_s, *here)
    there = {k: hop(q[k], lambda i: X) for k in order[:2]}
    sums = kernel_call(of_e, [wide] * 6, flags, w_e, found, *here)
    there[order[2]] = hop(q[order[2]], lambda i: X)
    leave, stay = sums[:3], sums[3:]

    turn = (sums,)
    r, swap, across, back_in = {}, {}, {}, {}
    totals, kept, done, results = {}, {}, {}, {}

    def take(value):
        return after(value, turn)

    def leave_stage(k):
        p_got, q_got = p_in[k], take(there[k])
        out = (leave[k] + jnp.where(even, q_got, p_got).astype(F32)).astype(BF16)
        r[k] = hop(out, lambda i: Y)
        totals[k] = stay[k] + jnp.where(even, p_got, q_got).astype(F32)
        totals[k] = lax.optimization_barrier(totals[k])
        return out

    def swap_stage(k):
        total = totals[k] + take(r[k]).astype(F32)
        upper, lower = total[:half], total[half:]
        out = jnp.where(keep_low, lower, upper).astype(BF16)
        kept[k] = jnp.where(keep_low, upper, lower)
        swap[k] = along(out, PAIRS)
        return out

    def across_stage(k):
        kept[k] = lax.reduce_precision(kept[k] + take(swap[k]).astype(F32), 8, 7)
        out = kept[k].astype(BF16)
        across[k] = along(out, ACROSS)
        return out

    def back_stage(k):
        done[k] = (kept[k] + take(across[k]).astype(F32)).astype(BF16)
        back_in[k] = along(done[k], PAIRS)
        return done[k]

    def result_stage(k):
        mine, got = done[k], take(back_in[k])
        results[k] = jnp.concatenate(
            [jnp.where(keep_low, mine, got), jnp.where(keep_low, got, mine)]
        )
        return results[k]

    stages = [leave_stage, swap_stage, across_stage, back_stage, result_stage]
    steps = ((0, 0), (1, 0), (0, 1), (2, 0), (1, 1), (0, 2), (2, 1), (1, 2), (2, 2), (0, 3), (1, 3), (2, 3), (0, 4), (1, 4), (2, 4))
    for k, at in steps:
        turn = stages[at](order[k])
    return results[0], results[1], results[2]


def solution(mesh):
    fits = mesh.shape["section"] == 8 and mesh.shape["dp"] == 4
    return jax.shard_map(
        square if fits else ring,
        mesh=mesh,
        in_specs=(
            P(("section", "dp"), None),
            P(("section", "dp"), None),
            P("section", None),
            P("section", None),
            P("section", None),
        ),
        out_specs=(P("section", None), P("section", None), P("section", None)),
        check_vma=False,
    )
```
